32 devices in a mesh: dp: 4 (over y, x), tensor: 8 (over z, core).
Axes of the slice: x: 2, y: 2, z: 4, core: 2. Of those that a mesh axis runs over, the one named last changes fastest.
Arguments:
- grad_out: bfloat16 [64, 8192], P('dp'), may hold values from -6 to 6
- gate_act: bfloat16 [64, 1408], P('dp', 'tensor'), may hold values from -6 to 6
- up_act: bfloat16 [64, 1408], P('dp', 'tensor'), may hold values from -6 to 6
- w_gate: bfloat16 [1408, 8192], P('tensor'), may hold values from -0.0625 to 0.0625
- w_up: bfloat16 [1408, 8192], P('tensor'), may hold values from -0.0625 to 0.0625
- w_down: bfloat16 [1408, 8192], P('tensor'), may hold values from -0.15625 to 0.15625
Outputs:
- input_grad: bfloat16 [64, 8192], P(('dp', 'tensor'))
- down_grad: bfloat16 [1408, 8192], P('tensor', 'dp')
The draws below stay inside these ranges and needn't reach their ends.
All inputs are finite; a program needn't handle non-finite values.
Results may differ from the reference program's by a relative error of at most 0.014.
Values may be sent and summed in bfloat16 or wider, within the bound.
A program may use at most 64 MiB of HBM per device.

```python
import jax
import jax.numpy as jnp
from jax import lax

D = 8192
FF = 1408
GROUP = 16
TOKENS = 64
N_DP = 4


def raised(entries, key, source, target, parts, factor):
    def block_of(position):
        return (jnp.arange(entries.shape[position]) // (entries.shape[position] // parts)).reshape((-1,) + (1,) * (entries.ndim - 1 - position))

    first = jax.random.permutation(key, parts)[block_of(target)]
    second = (block_of(target) + parts // 2) % parts
    return jnp.where((block_of(source) == first) | (block_of(source) == second), factor * entries, entries)


def levels(rng, dims, shards, smallest, largest):
    def one(position, blocks):
        heights = jax.random.uniform(jax.random.fold_in(jax.random.fold_in(rng, 6), position), (blocks,), jnp.float32, smallest / len(shards), largest / len(shards))
        return jnp.repeat(jnp.exp(heights), dims[position] // blocks).reshape((-1,) + (1,) * (len(dims) - position - 1))

    gain = one(*shards[0])
    for cut in shards[1:]:
        gain = gain * one(*cut)
    return gain


def normal_values(rng, shape, deviation, most, pieces=(), kind=jnp.bfloat16):
    array = deviation * jax.random.normal(rng, shape, jnp.float32)
    if pieces:
        array = array * levels(rng, shape, pieces, -0.22, 0.18)
    return jnp.clip(array, -most, most).astype(kind)


def noise_with(rng, extent, spread, most, shards, heavy, held_as=jnp.bfloat16):
    result = spread * jax.random.normal(rng, extent, jnp.float32)
    if shards:
        result = result * levels(rng, extent, shards, -0.22, 0.18)
    return jnp.clip(raised(result, jax.random.fold_in(rng, 3), *heavy), -most, most).astype(held_as)


def setup_inputs(seed: int = 0) -> dict:
    key_list = jax.random.split(jax.random.key(seed), 7)
    return {
        "grad_out": noise_with(key_list[0], (TOKENS, D), 1.0, 6.0, ((0, 4),), (0, 1, 4, 2.0)),
        "gate_act": noise_with(key_list[1], (TOKENS, FF), 1.0, 6.0, ((0, 4), (1, 8)), (1, 0, 8, 2.0)),
        "up_act": normal_values(key_list[2], (TOKENS, FF), 1.0, 6.0, ((0, 4), (1, 8))),
        "w_gate": normal_values(key_list[3], (FF, D), D ** -0.5, 0.0625, ((0, 8),)),
        "w_up": normal_values(key_list[4], (FF, D), D ** -0.5, 0.0625, ((0, 8),)),
        "w_down": normal_values(key_list[5], (FF, D), FF ** -0.5, 0.15625, ((0, 8),)),
    }


def reference(grad_out, gate_act, up_act, w_gate, w_up, w_down):
    gate = gate_act.astype(jnp.float32)
    up = up_act.astype(jnp.float32)
    sig = jax.nn.sigmoid(gate)
    silu = gate * sig
    hidden = (silu * up).astype(jnp.bfloat16)
    hidden_grad = lax.dot_general(grad_out, w_down, (((1,), (1,)), ((), ())), preferred_element_type=jnp.float32)
    gate_grad = (hidden_grad * up * sig * (1.0 + gate * (1.0 - sig))).astype(jnp.bfloat16)
    up_grad = (hidden_grad * silu).astype(jnp.bfloat16)
    input_grad = (jnp.dot(gate_grad, w_gate, preferred_element_type=jnp.float32)
                  + jnp.dot(up_grad, w_up, preferred_element_type=jnp.float32)).astype(jnp.bfloat16)
    hidden_groups = hidden.reshape(N_DP, GROUP, FF)
    grad_groups = grad_out.reshape(N_DP, GROUP, D)

    def accumulate(total, pair):
        part = lax.dot_general(pair[0], pair[1], (((0,), (0,)), ((), ())), preferred_element_type=jnp.float32)
        return total + part.astype(jnp.bfloat16).astype(jnp.float32), 0

    total, unused = lax.scan(accumulate, jnp.zeros((FF, D), jnp.float32), (hidden_groups, grad_groups))
    return input_grad, total.astype(jnp.bfloat16)
```

```python
import functools

import jax
import jax.numpy as jnp
from jax import lax
from jax.experimental import pallas as pl
from jax.experimental.pallas import tpu as pltpu
from jax.sharding import PartitionSpec as P

MESH = pl.DeviceIdType.MESH
PARTS = 4
F32 = jnp.float32
BF16 = jnp.bfloat16


def kernel(n_dp, n_t, g_hbm, gate_hbm, up_hbm, wg_hbm, wu_hbm, wd_hbm, ig_hbm, dg_hbm,
           g, gate_v, up_v, wg, wu, wd, g_all, h_all, to_pair, from_pair, mine, to_chips, from_chips,
           ig, dg, in_sem, wg_sem, wu_sem, wd_sem, own_sem, gs_sem, gr_sem, hs_sem, hr_sem,
           ps_sem, pr_sem, zs_sem, zr_sem, out_sem):
    tokens, width = g.shape
    units = gate_v.shape[1]
    chips = n_t // 2
    rows = tokens // n_t
    half = tokens // 2
    piece = width // PARTS
    cut = width // n_dp
    i = lax.axis_index("dp")
    t = lax.axis_index("tensor")
    chip, core = t // 2, lax.rem(t, 2)
    pair = t + 1 - 2 * core

    def chip_at(q):
        return 2 * lax.rem(chip + q, chips) + core

    def row_at(q):
        return lax.rem(i + q, n_dp)

    loads = [
        pltpu.make_async_copy(gate_hbm, gate_v, in_sem.at[0]),
        pltpu.make_async_copy(up_hbm, up_v, in_sem.at[1]),
        pltpu.make_async_copy(g_hbm, g, in_sem.at[2]),
    ]
    own = pltpu.make_async_copy(
        g_hbm.at[:, pl.ds(pl.multiple_of(i * cut, cut), cut)], g_all.at[pl.ds(0, tokens)], own_sem
    )
    weights = []
    for source, target, sem in ((wd_hbm, wd, wd_sem), (wg_hbm, wg, wg_sem), (wu_hbm, wu, wu_sem)):
        weights.append([
            pltpu.make_async_copy(source.at[:, pl.ds(k * piece, piece)], target.at[k], sem.at[k])
            for k in range(PARTS)
        ])
    wd_loads, wg_loads, wu_loads = weights
    for copy in loads + wd_loads:
        copy.start()

    barrier = pltpu.get_barrier_semaphore()
    pl.semaphore_signal(barrier, inc=1, device_id=(i, pair), device_id_type=MESH)
    for q in range(1, chips):
        pl.semaphore_signal(barrier, inc=1, device_id=(i, chip_at(q)), device_id_type=MESH)
    for q in range(1, n_dp):
        pl.semaphore_signal(barrier, inc=1, device_id=(row_at(q), t), device_id_type=MESH)

    for k in range(PARTS):
        wg_loads[k].start()
        wu_loads[k].start()
    own.start()

    loads[0].wait()
    loads[1].wait()
    gate = gate_v[...].astype(F32)
    up = up_v[...].astype(F32)
    sig = jax.nn.sigmoid(gate)
    silu = gate * sig
    h_all[pl.ds(0, tokens), :] = (silu * up).astype(BF16)

    pl.semaphore_wait(barrier, chips + n_dp - 1)
    gathers = []
    for q in range(1, n_dp):
        there = row_at(q)
        gathers.append(pltpu.make_async_remote_copy(
            src_ref=g_hbm.at[:, pl.ds(pl.multiple_of(there * cut, cut), cut)],
            dst_ref=g_all.at[pl.ds(q * tokens, tokens)],
            send_sem=gs_sem.at[q - 1], recv_sem=gr_sem.at[q - 1],
            device_id=(there, t), device_id_type=MESH,
        ))
        gathers.append(pltpu.make_async_remote_copy(
            src_ref=h_all.at[pl.ds(0, tokens)],
            dst_ref=h_all.at[pl.ds(q * tokens, tokens)],
            send_sem=hs_sem.at[q - 1], recv_sem=hr_sem.at[q - 1],
            device_id=(there, t), device_id_type=MESH,
        ))
    for copy in gathers:
        copy.start()

    loads[2].wait()
    hg = jnp.zeros((tokens, units), F32)
    for k in range(PARTS):
        wd_loads[k].wait()
        hg = hg + lax.dot_general(
            g[:, k * piece:(k + 1) * piece], wd[k], (((1,), (1,)), ((), ())), preferred_element_type=F32
        )
    gg = (hg * up * sig * (1.0 + gate * (1.0 - sig))).astype(BF16)
    ug = (hg * silu).astype(BF16)

    place = lax.broadcasted_iota(jnp.int32, (tokens, tokens), 0)
    token = lax.broadcasted_iota(jnp.int32, (tokens, tokens), 1)
    ours = (place >= half).astype(jnp.int32)
    inner = place - ours * half
    hop = inner // rows
    side = jnp.where(ours == 1, core, 1 - core)
    at_chip = chip + hop
    at_chip = jnp.where(at_chip >= chips, at_chip - chips, at_chip)
    wanted = (2 * at_chip + side) * rows + (inner - hop * rows)
    order = (wanted == token).astype(F32).astype(BF16)
    gg = jnp.dot(order, gg, preferred_element_type=F32).astype(BF16)
    ug = jnp.dot(order, ug, preferred_element_type=F32).astype(BF16)

    pair_copies = [
        pltpu.make_async_remote_copy(
            src_ref=to_pair.at[k], dst_ref=from_pair.at[k],
            send_sem=ps_sem.at[k], recv_sem=pr_sem.at[k],
            device_id=(i, pair), device_id_type=MESH,
        )
        for k in range(PARTS)
    ]

    def produce(k):
        wg_loads[k].wait()
        wu_loads[k].wait()
        terms = jnp.dot(gg, wg[k], preferred_element_type=F32) + jnp.dot(ug, wu[k], preferred_element_type=F32)
        to_pair[k] = terms[:half]
        pair_copies[k].start()
        mine[k] = terms[half:]

    def forward(k):
        pair_copies[k].wait_recv()
        mine[k] = mine[k] + from_pair[k]
        for q in range(1, chips):
            to_chips[k, q - 1] = mine[k, q * rows:(q + 1) * rows, :].astype(BF16)
        for q in range(1, chips):
            pltpu.make_async_remote_copy(
                src_ref=to_chips.at[k, q - 1], dst_ref=from_chips.at[k, q - 1],
                send_sem=zs_sem.at[k], recv_sem=zr_sem.at[k],
                device_id=(i, chip_at(q)), device_id_type=MESH,
            ).start()

    for k in range(PARTS):
        produce(k)
        if k > 0:
            forward(k - 1)
    forward(PARTS - 1)

    for copy in gathers:
        copy.wait_recv()
    own.wait()
    dg[...] = lax.dot_general(
        h_all[...], g_all[...], (((0,), (0,)), ((), ())), preferred_element_type=F32
    ).astype(BF16)
    dg_store = pltpu.make_async_copy(dg, dg_hbm, out_sem.at[0])
    dg_store.start()

    for k in range(PARTS):
        pltpu.make_async_copy(from_chips.at[k], from_chips.at[k], zr_sem.at[k]).wait()
        total = mine[k, 0:rows, :]
        for q in range(1, chips):
            total = total + from_chips[k, q - 1].astype(F32)
        ig[:, k * piece:(k + 1) * piece] = total.astype(BF16)
    ig_store = pltpu.make_async_copy(ig, ig_hbm, out_sem.at[1])
    ig_store.start()

    for copy in gathers + pair_copies:
        copy.wait_send()
    for k in range(PARTS):
        pltpu.make_async_copy(to_chips.at[k], to_chips.at[k], zs_sem.at[k]).wait()
    dg_store.wait()
    ig_store.wait()


def local(n_dp, n_t, grad_out, gate_act, up_act, w_gate, w_up, w_down):
    tokens, width = grad_out.shape
    units = gate_act.shape[1]
    chips, rows, half = n_t // 2, tokens // n_t, tokens // 2
    piece, cut = width // PARTS, width // n_dp
    dma = pltpu.SemaphoreType.DMA
    anywhere = pl.BlockSpec(memory_space=pl.ANY)
    return pl.pallas_call(
        functools.partial(kernel, n_dp, n_t),
        out_shape=(
            jax.ShapeDtypeStruct((rows, width), BF16),
            jax.ShapeDtypeStruct((units, cut), BF16),
        ),
        in_specs=[anywhere] * 6,
        out_specs=(anywhere, anywhere),
        scratch_shapes=[
            pltpu.VMEM((tokens, width), BF16),
            pltpu.VMEM((tokens, units), BF16),
            pltpu.VMEM((tokens, units), BF16),
            pltpu.VMEM((PARTS, units, piece), BF16),
            pltpu.VMEM((PARTS, units, piece), BF16),
            pltpu.VMEM((PARTS, units, piece), BF16),
            pltpu.VMEM((n_dp * tokens, cut), BF16),
            pltpu.VMEM((n_dp * tokens, units), BF16),
            pltpu.VMEM((PARTS, half, piece), F32),
            pltpu.VMEM((PARTS, half, piece), F32),
            pltpu.VMEM((PARTS, half, piece), F32),
            pltpu.VMEM((PARTS, chips - 1, rows, piece), BF16),
            pltpu.VMEM((PARTS, chips - 1, rows, piece), BF16),
            pltpu.VMEM((rows, width), BF16),
            pltpu.VMEM((units, cut), BF16),
            dma((3,)),
            dma((PARTS,)),
            dma((PARTS,)),
            dma((PARTS,)),
            dma,
            dma((n_dp - 1,)),
            dma((n_dp - 1,)),
            dma((n_dp - 1,)),
            dma((n_dp - 1,)),
            dma((PARTS,)),
            dma((PARTS,)),
            dma((PARTS,)),
            dma((PARTS,)),
            dma((2,)),
        ],
        compiler_params=pltpu.CompilerParams(
            collective_id=0, has_side_effects=True, vmem_limit_bytes=56 * 1024 * 1024
        ),
        cost_estimate=pl.CostEstimate(
            flops=2 * tokens * units * width * 4, bytes_accessed=3 * 2 * units * width, transcendentals=tokens * units
        ),
    )(grad_out, gate_act, up_act, w_gate, w_up, w_down)


def solution(mesh):
    placed = (
        P("dp", None),
        P("dp", "tensor"),
        P("dp", "tensor"),
        P("tensor", None),
        P("tensor", None),
        P("tensor", None),
    )
    return jax.shard_map(
        functools.partial(local, mesh.shape["dp"], mesh.shape["tensor"]),
        mesh=mesh,
        in_specs=placed,
        out_specs=(P(("dp", "tensor"), None), P("tensor", "dp")),
        check_vma=False,
    )
```

```python
import functools

import jax
import jax.numpy as jnp
from jax import lax
from jax.experimental import pallas as pl
from jax.experimental.pallas import tpu as pltpu
from jax.sharding import PartitionSpec as P

MESH = pl.DeviceIdType.MESH
PARTS = 4
F32 = jnp.float32
BF16 = jnp.bfloat16


def kernel(n_dp, n_t, g_hbm, gate_hbm, up_hbm, wg_hbm, wu_hbm, wd_hbm, ig, dg,
           g, gate_v, up_v, wg, wu, wd, g_all, h_all, to_pair, from_pair, mine, to_chips, from_chips,
           in_sem, wg_sem, wu_sem, wd_sem, own_sem, gs_sem, gr_sem, hs_sem, hr_sem,
           ps_sem, pr_sem, zs_sem, zr_sem):
    tokens, width = g.shape
    units = gate_v.shape[1]
    chips = n_t // 2
    rows = tokens // n_t
    half = tokens // 2
    piece = width // PARTS
    cut = width // n_dp
    i = lax.axis_index("dp")
    t = lax.axis_index("tensor")
    chip, core = t // 2, lax.rem(t, 2)
    pair = t + 1 - 2 * core

    def chip_at(q):
        return 2 * lax.rem(chip + q, chips) + core

    def row_at(q):
        return lax.rem(i + q, n_dp)

    loads = [
        pltpu.make_async_copy(gate_hbm, gate_v, in_sem.at[0]),
        pltpu.make_async_copy(up_hbm, up_v, in_sem.at[1]),
        pltpu.make_async_copy(g_hbm, g, in_sem.at[2]),
    ]
    own = pltpu.make_async_copy(
        g_hbm.at[:, pl.ds(pl.multiple_of(i * cut, cut), cut)], g_all.at[pl.ds(0, tokens)], own_sem
    )
    weights = []
    for source, target, sem in ((wd_hbm, wd, wd_sem), (wg_hbm, wg, wg_sem), (wu_hbm, wu, wu_sem)):
        weights.append([
            pltpu.make_async_copy(source.at[:, pl.ds(k * piece, piece)], target.at[k], sem.at[k])
            for k in range(PARTS)
        ])
    wd_loads, wg_loads, wu_loads = weights
    for copy in loads + wd_loads:
        copy.start()

    barrier = pltpu.get_barrier_semaphore()
    pl.semaphore_signal(barrier, inc=1, device_id=(i, pair), device_id_type=MESH)
    for q in range(1, chips):
        pl.semaphore_signal(barrier, inc=1, device_id=(i, chip_at(q)), device_id_type=MESH)
    for q in range(1, n_dp):
        pl.semaphore_signal(barrier, inc=1, device_id=(row_at(q), t), device_id_type=MESH)

    for k in range(PARTS):
        wg_loads[k].start()
        wu_loads[k].start()
    own.start()

    loads[0].wait()
    loads[1].wait()
    gate = gate_v[...].astype(F32)
    up = up_v[...].astype(F32)
    sig = jax.nn.sigmoid(gate)
    silu = gate * sig
    h_all[pl.ds(0, tokens), :] = (silu * up).astype(BF16)

    pl.semaphore_wait(barrier, chips + n_dp - 1)
    gathers = []
    for q in range(1, n_dp):
        there = row_at(q)
        gathers.append(pltpu.make_async_remote_copy(
            src_ref=g_hbm.at[:, pl.ds(pl.multiple_of(there * cut, cut), cut)],
            dst_ref=g_all.at[pl.ds(q * tokens, tokens)],
            send_sem=gs_sem.at[q - 1], recv_sem=gr_sem.at[q - 1],
            device_id=(there, t), device_id_type=MESH,
        ))
        gathers.append(pltpu.make_async_remote_copy(
            src_ref=h_all.at[pl.ds(0, tokens)],
            dst_ref=h_all.at[pl.ds(q * tokens, tokens)],
            send_sem=hs_sem.at[q - 1], recv_sem=hr_sem.at[q - 1],
            device_id=(there, t), device_id_type=MESH,
        ))
    for copy in gathers:
        copy.start()

    loads[2].wait()
    hg = jnp.zeros((tokens, units), F32)
    for k in range(PARTS):
        wd_loads[k].wait()
        hg = hg + lax.dot_general(
            g[:, k * piece:(k + 1) * piece], wd[k], (((1,), (1,)), ((), ())), preferred_element_type=F32
        )
    gg = (hg * up * sig * (1.0 + gate * (1.0 - sig))).astype(BF16)
    ug = (hg * silu).astype(BF16)

    place = lax.broadcasted_iota(jnp.int32, (tokens, tokens), 0)
    token = lax.broadcasted_iota(jnp.int32, (tokens, tokens), 1)
    ours = (place >= half).astype(jnp.int32)
    inner = place - ours * half
    hop = inner // rows
    side = jnp.where(ours == 1, core, 1 - core)
    at_chip = chip + hop
    at_chip = jnp.where(at_chip >= chips, at_chip - chips, at_chip)
    wanted = (2 * at_chip + side) * rows + (inner - hop * rows)
    order = (wanted == token).astype(F32).astype(BF16)
    gg = jnp.dot(order, gg, preferred_element_type=F32).astype(BF16)
    ug = jnp.dot(order, ug, preferred_element_type=F32).astype(BF16)

    pair_copies = [
        pltpu.make_async_remote_copy(
            src_ref=to_pair.at[k], dst_ref=from_pair.at[k],
            send_sem=ps_sem.at[k], recv_sem=pr_sem.at[k],
            device_id=(i, pair), device_id_type=MESH,
        )
        for k in range(PARTS)
    ]

    def produce(k):
        wg_loads[k].wait()
        wu_loads[k].wait()
        terms = jnp.dot(gg, wg[k], preferred_element_type=F32) + jnp.dot(ug, wu[k], preferred_element_type=F32)
        to_pair[k] = terms[:half]
        pair_copies[k].start()
        mine[k] = terms[half:]

    def forward(k):
        pair_copies[k].wait_recv()
        mine[k] = mine[k] + from_pair[k]
        for q in range(1, chips):
            to_chips[k, q - 1] = mine[k, q * rows:(q + 1) * rows, :].astype(BF16)
        for q in range(1, chips):
            pltpu.make_async_remote_copy(
                src_ref=to_chips.at[k, q - 1], dst_ref=from_chips.at[k, q - 1],
                send_sem=zs_sem.at[k], recv_sem=zr_sem.at[k],
                device_id=(i, chip_at(q)), device_id_type=MESH,
            ).start()

    for k in range(PARTS):
        produce(k)
        if k > 0:
            forward(k - 1)
    forward(PARTS - 1)

    for copy in gathers:
        copy.wait_recv()
    own.wait()
    dg[...] = lax.dot_general(
        h_all[...], g_all[...], (((0,), (0,)), ((), ())), preferred_element_type=F32
    ).astype(BF16)

    for k in range(PARTS):
        pltpu.make_async_copy(from_chips.at[k], from_chips.at[k], zr_sem.at[k]).wait()
        total = mine[k, 0:rows, :]
        for q in range(1, chips):
            total = total + from_chips[k, q - 1].astype(F32)
        ig[:, k * piece:(k + 1) * piece] = total.astype(BF16)

    for copy in gathers + pair_copies:
        copy.wait_send()
    for k in range(PARTS):
        pltpu.make_async_copy(to_chips.at[k], to_chips.at[k], zs_sem.at[k]).wait()


def place_kernel(ig, dg, ig_hbm, dg_hbm, sem):
    copies = [
        pltpu.make_async_copy(dg, dg_hbm, sem.at[0]),
        pltpu.make_async_copy(ig, ig_hbm, sem.at[1]),
    ]
    for copy in copies:
        copy.start()
    for copy in copies:
        copy.wait()


def local(n_dp, n_t, grad_out, gate_act, up_act, w_gate, w_up, w_down):
    tokens, width = grad_out.shape
    units = gate_act.shape[1]
    chips, rows, half = n_t // 2, tokens // n_t, tokens // 2
    piece, cut = width // PARTS, width // n_dp
    dma = pltpu.SemaphoreType.DMA
    anywhere = pl.BlockSpec(memory_space=pl.ANY)
    held = pl.pallas_call(
        functools.partial(kernel, n_dp, n_t),
        out_shape=(
            pltpu.VMEM((rows, width), BF16),
            pltpu.VMEM((units, cut), BF16),
        ),
        in_specs=[anywhere] * 6,
        out_specs=(pl.BlockSpec(memory_space=pltpu.VMEM),) * 2,
        scratch_shapes=[
            pltpu.VMEM((tokens, width), BF16),
            pltpu.VMEM((tokens, units), BF16),
            pltpu.VMEM((tokens, units), BF16),
            pltpu.VMEM((PARTS, units, piece), BF16),
            pltpu.VMEM((PARTS, units, piece), BF16),
            pltpu.VMEM((PARTS, units, piece), BF16),
            pltpu.VMEM((n_dp * tokens, cut), BF16),
            pltpu.VMEM((n_dp * tokens, units), BF16),
            pltpu.VMEM((PARTS, half, piece), F32),
            pltpu.VMEM((PARTS, half, piece), F32),
            pltpu.VMEM((PARTS, half, piece), F32),
            pltpu.VMEM((PARTS, chips - 1, rows, piece), BF16),
            pltpu.VMEM((PARTS, chips - 1, rows, piece), BF16),
            dma((3,)),
            dma((PARTS,)),
            dma((PARTS,)),
            dma((PARTS,)),
            dma,
            dma((n_dp - 1,)),
            dma((n_dp - 1,)),
            dma((n_dp - 1,)),
            dma((n_dp - 1,)),
            dma((PARTS,)),
            dma((PARTS,)),
            dma((PARTS,)),
            dma((PARTS,)),
        ],
        compiler_params=pltpu.CompilerParams(
            collective_id=0, has_side_effects=True, vmem_limit_bytes=56 * 1024 * 1024
        ),
        cost_estimate=pl.CostEstimate(
            flops=2 * tokens * units * width * 4, bytes_accessed=3 * 2 * units * width, transcendentals=tokens * units
        ),
    )(grad_out, gate_act, up_act, w_gate, w_up, w_down)
    held = [pltpu.with_memory_space_constraint(x, pltpu.VMEM) for x in held]
    return pl.pallas_call(
        place_kernel,
        out_shape=(
            jax.ShapeDtypeStruct((rows, width), BF16),
            jax.ShapeDtypeStruct((units, cut), BF16),
        ),
        in_specs=[pl.BlockSpec(memory_space=pltpu.VMEM)] * 2,
        out_specs=(anywhere, anywhere),
        scratch_shapes=[dma((2,))],
    )(*held)


def solution(mesh):
    placed = (
        P("dp", None),
        P("dp", "tensor"),
        P("dp", "tensor"),
        P("tensor", None),
        P("tensor", None),
        P("tensor", None),
    )
    return jax.shard_map(
        functools.partial(local, mesh.shape["dp"], mesh.shape["tensor"]),
        mesh=mesh,
        in_specs=placed,
        out_specs=(P(("dp", "tensor"), None), P("tensor", "dp")),
        check_vma=False,
    )
```

```python
import functools

import jax
import jax.numpy as jnp
from jax import lax
from jax.experimental import pallas as pl
from jax.experimental.pallas import tpu as pltpu
from jax.sharding import PartitionSpec as P

MESH = pl.DeviceIdType.MESH
PARTS = 2
STEPS = 4
F32 = jnp.float32
BF16 = jnp.bfloat16


def kernel(n_dp, n_t, g_hbm, gate_hbm, up_hbm, wg_hbm, wu_hbm, wd_hbm, ig, dg,
           g, gate_v, up_v, wg, wu, wd, g_all, h_all, to_pair, from_pair, mine, to_chips, from_chips,
           in_sem, wg_sem, wu_sem, wd_sem, own_sem, gs_sem, gr_sem, hs_sem, hr_sem,
           ps_sem, pr_sem, zs_sem, zr_sem):
    tokens, width = g.shape
    units = gate_v.shape[1]
    chips = n_t // 2
    rows = tokens // n_t
    half = tokens // 2
    piece = width // PARTS
    step = width // STEPS
    cut = width // n_dp
    i = lax.axis_index("dp")
    t = lax.axis_index("tensor")
    chip, core = t // 2, lax.rem(t, 2)
    pair = t + 1 - 2 * core

    def chip_at(q):
        return 2 * lax.rem(chip + q, chips) + core

    def row_at(q):
        return lax.rem(i + q, n_dp)

    loads = [
        pltpu.make_async_copy(gate_hbm, gate_v, in_sem.at[0]),
        pltpu.make_async_copy(up_hbm, up_v, in_sem.at[1]),
        pltpu.make_async_copy(g_hbm, g, in_sem.at[2]),
    ]
    own = pltpu.make_async_copy(
        g_hbm.at[:, pl.ds(pl.multiple_of(i * cut, cut), cut)], g_all.at[pl.ds(0, tokens)], own_sem
    )
    weights = []
    for source, target, sem, wide in (
        (wd_hbm, wd, wd_sem, step), (wg_hbm, wg, wg_sem, piece), (wu_hbm, wu, wu_sem, piece)
    ):
        weights.append([
            pltpu.make_async_copy(source.at[:, pl.ds(k * wide, wide)], target.at[k], sem.at[k])
            for k in range(width // wide)
        ])
    wd_loads, wg_loads, wu_loads = weights
    for copy in loads + wd_loads:
        copy.start()

    barrier = pltpu.get_barrier_semaphore()
    pl.semaphore_signal(barrier, inc=1, device_id=(i, pair), device_id_type=MESH)
    for q in range(1, chips):
        pl.semaphore_signal(barrier, inc=1, device_id=(i, chip_at(q)), device_id_type=MESH)
    for q in range(1, n_dp):
        pl.semaphore_signal(barrier, inc=1, device_id=(row_at(q), t), device_id_type=MESH)

    for k in range(PARTS):
        wg_loads[k].start()
        wu_loads[k].start()
    own.start()

    loads[0].wait()
    loads[1].wait()
    gate = gate_v[...].astype(F32)
    up = up_v[...].astype(F32)
    sig = jax.nn.sigmoid(gate)
    silu = gate * sig
    h_all[pl.ds(0, tokens), :] = (silu * up).astype(BF16)

    place = lax.broadcasted_iota(jnp.int32, (tokens, tokens), 0)
    token = lax.broadcasted_iota(jnp.int32, (tokens, tokens), 1)
    ours = (place >= half).astype(jnp.int32)
    inner = place - ours * half
    hop = inner // rows
    side = jnp.where(ours == 1, core, 1 - core)
    at_chip = chip + hop
    at_chip = jnp.where(at_chip >= chips, at_chip - chips, at_chip)
    wanted = (2 * at_chip + side) * rows + (inner - hop * rows)
    order = (wanted == token).astype(F32).astype(BF16)
    gate = jnp.dot(order, gate_v[...], preferred_element_type=F32)
    up = jnp.dot(order, up_v[...], preferred_element_type=F32)
    sig = jax.nn.sigmoid(gate)
    silu = gate * sig
    gate_factor = up * sig * (1.0 + gate * (1.0 - sig))

    gathers = []
    for q in range(1, n_dp):
        there = row_at(q)
        gathers.append(pltpu.make_async_remote_copy(
            src_ref=g_hbm.at[:, pl.ds(pl.multiple_of(there * cut, cut), cut)],
            dst_ref=g_all.at[pl.ds(q * tokens, tokens)],
            send_sem=gs_sem.at[q - 1], recv_sem=gr_sem.at[q - 1],
            device_id=(there, t), device_id_type=MESH,
        ))
        gathers.append(pltpu.make_async_remote_copy(
            src_ref=h_all.at[pl.ds(0, tokens)],
            dst_ref=h_all.at[pl.ds(q * tokens, tokens)],
            send_sem=hs_sem.at[q - 1], recv_sem=hr_sem.at[q - 1],
            device_id=(there, t), device_id_type=MESH,
        ))

    loads[2].wait()
    for k in range(STEPS):
        part = slice(k * step, (k + 1) * step)
        g[:, part] = jnp.dot(order, g[:, part], preferred_element_type=F32).astype(BF16)
    sums = [jnp.zeros((tokens, units), F32) for _ in range(4)]
    for k in range(STEPS):
        wd_loads[k].wait()
        for n in range(4):
            quarter = step // 4
            sums[n] = sums[n] + lax.dot_general(
                g[:, k * step + n * quarter:k * step + (n + 1) * quarter], wd[k, :, n * quarter:(n + 1) * quarter],
                (((1,), (1,)), ((), ())), preferred_element_type=F32
            )
        if k == 1:
            pl.semaphore_wait(barrier, chips + n_dp - 1)
            for copy in gathers:
                copy.start()
    hg = (sums[0] + sums[1]) + (sums[2] + sums[3])

    gg = (hg * gate_factor).astype(BF16)
    ug = (hg * silu).astype(BF16)

    pair_copies = [
        pltpu.make_async_remote_copy(
            src_ref=to_pair.at[k], dst_ref=from_pair.at[k],
            send_sem=ps_sem.at[k], recv_sem=pr_sem.at[k],
            device_id=(i, pair), device_id_type=MESH,
        )
        for k in range(PARTS)
    ]

    def produce(k):
        wg_loads[k].wait()
        wu_loads[k].wait()
        terms = jnp.dot(gg, wg[k], preferred_element_type=F32) + jnp.dot(ug, wu[k], preferred_element_type=F32)
        to_pair[k] = terms[:half]
        pair_copies[k].start()
        mine[k] = terms[half:]

    def forward(k):
        pair_copies[k].wait_recv()
        mine[k] = mine[k] + from_pair[k]
        for q in range(1, chips):
            to_chips[k, q - 1] = mine[k, q * rows:(q + 1) * rows, :].astype(BF16)
        for q in range(1, chips):
            pltpu.make_async_remote_copy(
                src_ref=to_chips.at[k, q - 1], dst_ref=from_chips.at[k, q - 1],
                send_sem=zs_sem.at[k], recv_sem=zr_sem.at[k],
                device_id=(i, chip_at(q)), device_id_type=MESH,
            ).start()

    for k in range(PARTS):
        produce(k)
        if k > 0:
            forward(k - 1)
    forward(PARTS - 1)

    for copy in gathers:
        copy.wait_recv()
    own.wait()
    dg[...] = lax.dot_general(
        h_all[...], g_all[...], (((0,), (0,)), ((), ())), preferred_element_type=F32
    ).astype(BF16)

    for k in range(PARTS):
        pltpu.make_async_copy(from_chips.at[k], from_chips.at[k], zr_sem.at[k]).wait()
        total = mine[k, 0:rows, :]
        for q in range(1, chips):
            total = total + from_chips[k, q - 1].astype(F32)
        ig[:, k * piece:(k + 1) * piece] = total.astype(BF16)

    for copy in gathers + pair_copies:
        copy.wait_send()
    for k in range(PARTS):
        pltpu.make_async_copy(to_chips.at[k], to_chips.at[k], zs_sem.at[k]).wait()


def place_kernel(ig, dg, ig_hbm, dg_hbm, sem):
    copies = [
        pltpu.make_async_copy(dg, dg_hbm, sem.at[0]),
        pltpu.make_async_copy(ig, ig_hbm, sem.at[1]),
    ]
    for copy in copies:
        copy.start()
    for copy in copies:
        copy.wait()


def local(n_dp, n_t, grad_out, gate_act, up_act, w_gate, w_up, w_down):
    tokens, width = grad_out.shape
    units = gate_act.shape[1]
    chips, rows, half = n_t // 2, tokens // n_t, tokens // 2
    piece, step, cut = width // PARTS, width // STEPS, width // n_dp
    dma = pltpu.SemaphoreType.DMA
    anywhere = pl.BlockSpec(memory_space=pl.ANY)
    held = pl.pallas_call(
        functools.partial(kernel, n_dp, n_t),
        out_shape=(
            pltpu.VMEM((rows, width), BF16),
            pltpu.VMEM((units, cut), BF16),
        ),
        in_specs=[anywhere] * 6,
        out_specs=(pl.BlockSpec(memory_space=pltpu.VMEM),) * 2,
        scratch_shapes=[
            pltpu.VMEM((tokens, width), BF16),
            pltpu.VMEM((tokens, units), BF16),
            pltpu.VMEM((tokens, units), BF16),
            pltpu.VMEM((PARTS, units, piece), BF16),
            pltpu.VMEM((PARTS, units, piece), BF16),
            pltpu.VMEM((STEPS, units, step), BF16),
            pltpu.VMEM((n_dp * tokens, cut), BF16),
            pltpu.VMEM((n_dp * tokens, units), BF16),
            pltpu.VMEM((PARTS, half, piece), F32),
            pltpu.VMEM((PARTS, half, piece), F32),
            pltpu.VMEM((PARTS, half, piece), F32),
            pltpu.VMEM((PARTS, chips - 1, rows, piece), BF16),
            pltpu.VMEM((PARTS, chips - 1, rows, piece), BF16),
            dma((3,)),
            dma((PARTS,)),
            dma((PARTS,)),
            dma((STEPS,)),
            dma,
            dma((n_dp - 1,)),
            dma((n_dp - 1,)),
            dma((n_dp - 1,)),
            dma((n_dp - 1,)),
            dma((PARTS,)),
            dma((PARTS,)),
            dma((PARTS,)),
            dma((PARTS,)),
        ],
        compiler_params=pltpu.CompilerParams(
            collective_id=0, has_side_effects=True, vmem_limit_bytes=56 * 1024 * 1024
        ),
        cost_estimate=pl.CostEstimate(
            flops=2 * tokens * units * width * 4, bytes_accessed=3 * 2 * units * width, transcendentals=tokens * units
        ),
    )(grad_out, gate_act, up_act, w_gate, w_up, w_down)
    held = [pltpu.with_memory_space_constraint(x, pltpu.VMEM) for x in held]
    return pl.pallas_call(
        place_kernel,
        out_shape=(
            jax.ShapeDtypeStruct((rows, width), BF16),
            jax.ShapeDtypeStruct((units, cut), BF16),
        ),
        in_specs=[pl.BlockSpec(memory_space=pltpu.VMEM)] * 2,
        out_specs=(anywhere, anywhere),
        scratch_shapes=[dma((2,))],
    )(*held)


def solution(mesh):
    placed = (
        P("dp", None),
        P("dp", "tensor"),
        P("dp", "tensor"),
        P("tensor", None),
        P("tensor", None),
        P("tensor", None),
    )
    return jax.shard_map(
        functools.partial(local, mesh.shape["dp"], mesh.shape["tensor"]),
        mesh=mesh,
        in_specs=placed,
        out_specs=(P(("dp", "tensor"), None), P("tensor", "dp")),
        check_vma=False,
    )
```

```python
import functools

import jax
import jax.numpy as jnp
from jax import lax
from jax.experimental import pallas as pl
from jax.experimental.pallas import tpu as pltpu
from jax.sharding import PartitionSpec as P

MESH = pl.DeviceIdType.MESH
PARTS = 2
STEPS = 4
F32 = jnp.float32
BF16 = jnp.bfloat16


def kernel(n_dp, n_t, g_hbm, gate_hbm, up_hbm, wg_hbm, wu_hbm, wd_hbm, ig, dg,
           g, gate_v, up_v, wg, wu, wd, g_all, h_all, to_pair, from_pair, mine, to_chips, from_chips,
           in_sem, wg_sem, wu_sem, wd_sem, own_sem, gs_sem, gr_sem, hs_sem, hr_sem,
           ps_sem, pr_sem, zs_sem, zr_sem):
    tokens, width = g.shape
    units = gate_v.shape[1]
    chips = n_t // 2
    rows = tokens // n_t
    half = tokens // 2
    piece = width // PARTS
    step = width // STEPS
    cut = width // n_dp
    i = lax.axis_index("dp")
    t = lax.axis_index("tensor")
    chip, core = t // 2, lax.rem(t, 2)
    pair = t + 1 - 2 * core

    def chip_at(q):
        return 2 * lax.rem(chip + q, chips) + core

    def row_at(q):
        return lax.rem(i + q, n_dp)

    loads = [
        pltpu.make_async_copy(gate_hbm, gate_v, in_sem.at[0]),
        pltpu.make_async_copy(up_hbm, up_v, in_sem.at[1]),
        pltpu.make_async_copy(g_hbm, g, in_sem.at[2]),
    ]
    own = pltpu.make_async_copy(
        g_hbm.at[:, pl.ds(pl.multiple_of(i * cut, cut), cut)], g_all.at[pl.ds(0, tokens)], own_sem
    )
    weights = []
    for source, target, sem, wide in (
        (wd_hbm, wd, wd_sem, step), (wg_hbm, wg, wg_sem, piece), (wu_hbm, wu, wu_sem, piece)
    ):
        weights.append([
            pltpu.make_async_copy(source.at[:, pl.ds(k * wide, wide)], target.at[k], sem.at[k])
            for k in range(width // wide)
        ])
    wd_loads, wg_loads, wu_loads = weights
    for copy in loads + wd_loads:
        copy.start()

    barrier = pltpu.get_barrier_semaphore()
    pl.semaphore_signal(barrier, inc=1, device_id=(i, pair), device_id_type=MESH)
    for q in range(1, chips):
        pl.semaphore_signal(barrier, inc=1, device_id=(i, chip_at(q)), device_id_type=MESH)
    for q in range(1, n_dp):
        pl.semaphore_signal(barrier, inc=1, device_id=(row_at(q), t), device_id_type=MESH)

    for k in range(PARTS):
        wg_loads[k].start()
        wu_loads[k].start()
    own.start()

    loads[0].wait()
    loads[1].wait()
    gate = gate_v[...].astype(F32)
    up = up_v[...].astype(F32)
    sig = jax.nn.sigmoid(gate)
    silu = gate * sig
    h_all[pl.ds(0, tokens), :] = (silu * up).astype(BF16)

    place = lax.broadcasted_iota(jnp.int32, (tokens, tokens), 0)
    token = lax.broadcasted_iota(jnp.int32, (tokens, tokens), 1)
    ours = (place >= half).astype(jnp.int32)
    inner = place - ours * half
    hop = inner // rows
    side = jnp.where(ours == 1, core, 1 - core)
    at_chip = chip + hop
    at_chip = jnp.where(at_chip >= chips, at_chip - chips, at_chip)
    wanted = (2 * at_chip + side) * rows + (inner - hop * rows)
    order = (wanted == token).astype(F32).astype(BF16)
    gate = jnp.dot(order, gate_v[...], preferred_element_type=F32)
    up = jnp.dot(order, up_v[...], preferred_element_type=F32)
    sig = jax.nn.sigmoid(gate)
    silu = gate * sig
    gate_factor = up * sig * (1.0 + gate * (1.0 - sig))

    gathers = []
    for q in range(1, n_dp):
        there = row_at(q)
        gathers.append(pltpu.make_async_remote_copy(
            src_ref=g_hbm.at[:, pl.ds(pl.multiple_of(there * cut, cut), cut)],
            dst_ref=g_all.at[pl.ds(q * tokens, tokens)],
            send_sem=gs_sem.at[q - 1], recv_sem=gr_sem.at[q - 1],
            device_id=(there, t), device_id_type=MESH,
        ))
        gathers.append(pltpu.make_async_remote_copy(
            src_ref=h_all.at[pl.ds(0, tokens)],
            dst_ref=h_all.at[pl.ds(q * tokens, tokens)],
            send_sem=hs_sem.at[q - 1], recv_sem=hr_sem.at[q - 1],
            device_id=(there, t), device_id_type=MESH,
        ))

    loads[2].wait()
    for k in range(STEPS):
        part = slice(k * step, (k + 1) * step)
        g[:, part] = jnp.dot(order, g[:, part], preferred_element_type=F32).astype(BF16)
    sums = [jnp.zeros((tokens, units), F32) for _ in range(4)]
    for k in range(STEPS):
        wd_loads[k].wait()
        for n in range(4):
            quarter = step // 4
            sums[n] = sums[n] + lax.dot_general(
                g[:, k * step + n * quarter:k * step + (n + 1) * quarter], wd[k, :, n * quarter:(n + 1) * quarter],
                (((1,), (1,)), ((), ())), preferred_element_type=F32
            )
        if k == 1:
            pl.semaphore_wait(barrier, chips + n_dp - 1)
            for copy in gathers:
                copy.start()
    hg = (sums[0] + sums[1]) + (sums[2] + sums[3])

    gg = (hg * gate_factor).astype(BF16)
    ug = (hg * silu).astype(BF16)

    pair_copies = [
        pltpu.make_async_remote_copy(
            src_ref=to_pair.at[k], dst_ref=from_pair.at[k],
            send_sem=ps_sem.at[k], recv_sem=pr_sem.at[k],
            device_id=(i, pair), device_id_type=MESH,
        )
        for k in range(PARTS)
    ]

    def produce(k):
        wg_loads[k].wait()
        wu_loads[k].wait()
        terms = jnp.dot(gg, wg[k], preferred_element_type=F32) + jnp.dot(ug, wu[k], preferred_element_type=F32)
        to_pair[k] = terms[:half]
        pair_copies[k].start()
        mine[k] = terms[half:]

    def forward(k):
        pair_copies[k].wait_recv()
        for q in range(1, chips):
            lines = slice(q * rows, (q + 1) * rows)
            to_chips[k, q - 1] = (mine[k, lines, :] + from_pair[k, lines, :]).astype(BF16)
            pltpu.make_async_remote_copy(
                src_ref=to_chips.at[k, q - 1], dst_ref=from_chips.at[k, q - 1],
                send_sem=zs_sem.at[k], recv_sem=zr_sem.at[k],
                device_id=(i, chip_at(q)), device_id_type=MESH,
            ).start()

    for k in range(PARTS):
        produce(k)
        forward(k)

    for copy in gathers:
        copy.wait_recv()
    own.wait()
    dg[...] = lax.dot_general(
        h_all[...], g_all[...], (((0,), (0,)), ((), ())), preferred_element_type=F32
    ).astype(BF16)

    for k in range(PARTS):
        pltpu.make_async_copy(from_chips.at[k], from_chips.at[k], zr_sem.at[k]).wait()
        total = mine[k, 0:rows, :] + from_pair[k, 0:rows, :]
        for q in range(1, chips):
            total = total + from_chips[k, q - 1].astype(F32)
        ig[:, k * piece:(k + 1) * piece] = total.astype(BF16)

    for copy in gathers + pair_copies:
        copy.wait_send()
    for k in range(PARTS):
        pltpu.make_async_copy(to_chips.at[k], to_chips.at[k], zs_sem.at[k]).wait()


def place_kernel(ig, dg, ig_hbm, dg_hbm, sem):
    copies = [
        pltpu.make_async_copy(dg, dg_hbm, sem.at[0]),
        pltpu.make_async_copy(ig, ig_hbm, sem.at[1]),
    ]
    for copy in copies:
        copy.start()
    for copy in copies:
        copy.wait()


def local(n_dp, n_t, grad_out, gate_act, up_act, w_gate, w_up, w_down):
    tokens, width = grad_out.shape
    units = gate_act.shape[1]
    chips, rows, half = n_t // 2, tokens // n_t, tokens // 2
    piece, step, cut = width // PARTS, width // STEPS, width // n_dp
    dma = pltpu.SemaphoreType.DMA
    anywhere = pl.BlockSpec(memory_space=pl.ANY)
    held = pl.pallas_call(
        functools.partial(kernel, n_dp, n_t),
        out_shape=(
            pltpu.VMEM((rows, width), BF16),
            pltpu.VMEM((units, cut), BF16),
        ),
        in_specs=[anywhere] * 6,
        out_specs=(pl.BlockSpec(memory_space=pltpu.VMEM),) * 2,
        scratch_shapes=[
            pltpu.VMEM((tokens, width), BF16),
            pltpu.VMEM((tokens, units), BF16),
            pltpu.VMEM((tokens, units), BF16),
            pltpu.VMEM((PARTS, units, piece), BF16),
            pltpu.VMEM((PARTS, units, piece), BF16),
            pltpu.VMEM((STEPS, units, step), BF16),
            pltpu.VMEM((n_dp * tokens, cut), BF16),
            pltpu.VMEM((n_dp * tokens, units), BF16),
            pltpu.VMEM((PARTS, half, piece), F32),
            pltpu.VMEM((PARTS, half, piece), F32),
            pltpu.VMEM((PARTS, half, piece), F32),
            pltpu.VMEM((PARTS, chips - 1, rows, piece), BF16),
            pltpu.VMEM((PARTS, chips - 1, rows, piece), BF16),
            dma((3,)),
            dma((PARTS,)),
            dma((PARTS,)),
            dma((STEPS,)),
            dma,
            dma((n_dp - 1,)),
            dma((n_dp - 1,)),
            dma((n_dp - 1,)),
            dma((n_dp - 1,)),
            dma((PARTS,)),
            dma((PARTS,)),
            dma((PARTS,)),
            dma((PARTS,)),
        ],
        compiler_params=pltpu.CompilerParams(
            collective_id=0, has_side_effects=True, vmem_limit_bytes=56 * 1024 * 1024
        ),
        cost_estimate=pl.CostEstimate(
            flops=2 * tokens * units * width * 4, bytes_accessed=3 * 2 * units * width, transcendentals=tokens * units
        ),
    )(grad_out, gate_act, up_act, w_gate, w_up, w_down)
    held = [pltpu.with_memory_space_constraint(x, pltpu.VMEM) for x in held]
    return pl.pallas_call(
        place_kernel,
        out_shape=(
            jax.ShapeDtypeStruct((rows, width), BF16),
            jax.ShapeDtypeStruct((units, cut), BF16),
        ),
        in_specs=[pl.BlockSpec(memory_space=pltpu.VMEM)] * 2,
        out_specs=(anywhere, anywhere),
        scratch_shapes=[dma((2,))],
    )(*held)


def solution(mesh):
    placed = (
        P("dp", None),
        P("dp", "tensor"),
        P("dp", "tensor"),
        P("tensor", None),
        P("tensor", None),
        P("tensor", None),
    )
    return jax.shard_map(
        functools.partial(local, mesh.shape["dp"], mesh.shape["tensor"]),
        mesh=mesh,
        in_specs=placed,
        out_specs=(P(("dp", "tensor"), None), P("tensor", "dp")),
        check_vma=False,
    )
```
